32 devices in a mesh: leaf: 4 (over x, core), seq: 8 (over z, y).
Axes of the slice: x: 2, y: 2, z: 4, core: 2. Of those that a mesh axis runs over, the one named last changes fastest.
Arguments:
- tokens: bfloat16 [4, 1024, 2048], P('leaf', 'seq'), may hold values from -6 to 6
- parents: int32 [4, 13], P('leaf'), may hold values from 0 to 4, as said below
- lengths: int32 [4, 13], P('leaf'), may hold values from 1 to 512, as said below
- norm_attn: float32 [2048], P('seq'), may hold values from 0.5 to 1.5
- w_query: float32 [2048, 2048], P('seq'), may hold values from -0.125 to 0.125
- w_key: float32 [2048, 256], P('seq'), may hold values from -0.125 to 0.125
- w_value: float32 [2048, 256], P('seq'), may hold values from -0.125 to 0.125
- w_out: float32 [2048, 2048], P('seq'), may hold values from -2 to 2
- norm_ffn: float32 [2048], P('seq'), may hold values from 0.5 to 1.5
- w_gate: float32 [2048, 5632], P('seq'), may hold values from -0.125 to 0.125
- w_up: float32 [2048, 5632], P('seq'), may hold values from -0.125 to 0.125
- w_down: float32 [5632, 2048], P('seq'), may hold values from -0.078125 to 0.078125
- cotangent: bfloat16 [4, 1024, 2048], P('leaf', 'seq'), may hold values from -6 to 6
Outputs:
- output: bfloat16 [4, 1024, 2048], P('leaf', 'seq')
- input_grad: float32 [4, 1024, 2048], P('leaf', 'seq')
- grad_norm_attn: float32 [2048], P('seq')
- grad_query: float32 [2048, 2048], P('seq')
- grad_key: float32 [2048, 256], P('seq')
- grad_value: float32 [2048, 256], P('seq')
- grad_out: float32 [2048, 2048], P('seq')
- grad_norm_ffn: float32 [2048], P('seq')
- grad_gate: float32 [2048, 5632], P('seq')
- grad_up: float32 [2048, 5632], P('seq')
- grad_down: float32 [5632, 2048], P('seq')
The draws below stay inside these ranges and needn't reach their ends.
Inputs may be any that keep to these rules, and one draw needn't show every extreme that they name: In every tree segment 0 is the trunk and its own parent, segments 1 to 4 have parent 0, and segments after them are leaves whose parents are among 1 to 4, each branch the parent of 2 of them. In every tree the 13 lengths are positive and sum to 1024; segment 0 holds 512 tokens and is the longest.
All inputs are finite; a program needn't handle non-finite values.
Results may differ from the reference program's by a relative error of at most 0.022.
Values may be sent and summed in bfloat16 or wider, within the bound.
No kernel may reach another device: no remote copies, remote signals or barrier semaphores. Data moves between devices by JAX's collectives and lax.ppermute only.
A program may use at most 384 MiB of HBM per device.

```python
import jax
import jax.numpy as jnp
from jax import lax

D = 2048
HEADS = 32
KV_HEADS = 4
HEAD_DIM = 64
FF = 5632
BRANCHES = 4
LEAVES = 2
SEGS = 13
TREE_LEN = 1024
TREES = 4
KVW = 256


def draw_parents(key, part):
    leaf_parents = jnp.repeat(jnp.arange(1, BRANCHES + 1, dtype=jnp.int32), LEAVES)
    tree_keys = jax.random.split(key, TREES)
    shuffled = jax.vmap(lambda tree_key: jax.random.permutation(tree_key, leaf_parents))(tree_keys)
    heading = jnp.zeros((TREES, 1 + BRANCHES), jnp.int32)
    return jnp.concatenate([heading, shuffled], axis=1).astype(jnp.int32)


def draw_lengths(key, part):
    other_key = jax.random.fold_in(key, 17)
    trunk_len = TREE_LEN // 2
    weights = jax.random.randint(other_key, (TREES, SEGS - 1), 200, 1001).astype(jnp.int32)
    spare = TREE_LEN - trunk_len - (SEGS - 1)
    shares = 1 + weights * spare // jnp.sum(weights, axis=1, keepdims=True)
    missing = TREE_LEN - trunk_len - jnp.sum(shares, axis=1, keepdims=True)
    first_col = (jnp.arange(SEGS - 1, dtype=jnp.int32) == 0).astype(jnp.int32)
    others = shares + missing * first_col[None, :]
    trunk = jnp.full((TREES, 1), trunk_len, jnp.int32)
    return jnp.concatenate([trunk, others], axis=1).astype(jnp.int32)


def block_scale(own_key, extent, shards, smallest, largest):
    level, own = 1.0, jax.random.fold_in(own_key, 6)
    for dim, blocks in shards:
        heights = jnp.exp(jax.random.uniform(jax.random.fold_in(own, dim), (blocks,), jnp.float32, smallest / len(shards), largest / len(shards)))
        level = level * jnp.repeat(heights, extent[dim] // blocks).reshape([-1 if axis == dim else 1 for axis in range(len(extent))])
    return level


def bell_draw(own_key, shape, spread, most, cuts=(), kind=jnp.bfloat16):
    values = jax.random.normal(own_key, shape, jnp.float32) * spread
    if len(cuts) > 0:
        values = block_scale(own_key, shape, cuts, -0.22, 0.18) * values
    return jnp.clip(values, min=-most, max=most).astype(kind)


def setup_inputs(seed: int = 0) -> dict:
    arg_keys = jax.random.split(jax.random.key(seed), 14)
    return {
        "tokens": bell_draw(arg_keys[0], (TREES, TREE_LEN, D), 1.0, 6.0, ((0, 4), (1, 8))),
        "parents": draw_parents(jax.random.fold_in(arg_keys[13], 71), 0),
        "lengths": draw_lengths(jax.random.fold_in(arg_keys[13], 71), 0),
        "norm_attn": jnp.clip(1.0 + 0.1 * jax.random.normal(arg_keys[3], (D,), jnp.float32), 0.5, 1.5),
        "w_query": bell_draw(arg_keys[4], (D, D), D ** -0.5, 0.125, ((0, 8),), jnp.float32),
        "w_key": bell_draw(arg_keys[5], (D, KVW), D ** -0.5, 0.125, ((0, 8),), jnp.float32),
        "w_value": bell_draw(arg_keys[6], (D, KVW), D ** -0.5, 0.125, ((0, 8),), jnp.float32),
        "w_out": bell_draw(arg_keys[7], (D, D), 8 ** -0.5, 2.0, ((0, 8),), jnp.float32),
        "norm_ffn": jnp.clip(1.0 + 0.1 * jax.random.normal(arg_keys[8], (D,), jnp.float32), 0.5, 1.5),
        "w_gate": bell_draw(arg_keys[9], (D, FF), D ** -0.5, 0.125, ((0, 8),), jnp.float32),
        "w_up": bell_draw(arg_keys[10], (D, FF), D ** -0.5, 0.125, ((0, 8),), jnp.float32),
        "w_down": bell_draw(arg_keys[11], (FF, D), FF ** -0.5, 0.078125, ((0, 8),), jnp.float32),
        "cotangent": bell_draw(arg_keys[12], (TREES, TREE_LEN, D), 1.0, 6.0, ((0, 4), (1, 8))),
    }


@jax.custom_vjp
def low(v):
    return lax.optimization_barrier(v.astype(jnp.bfloat16)).astype(jnp.float32)

@jax.custom_vjp
def low_back(v):
    return v

def low_keep(v):
    return (low(v), None)

def low_pass(kept, grad):
    return (grad,)

def back_keep(v):
    return (v, None)

def back_low(kept, grad):
    return (low(grad),)
low.defvjp(low_keep, low_pass)
low_back.defvjp(back_keep, back_low)
EPSILON = 1e-05
NEGATIVE = -1e+30
THETA_BASE = 10000.0

def tree_layout(parent_row, length_row, tree_len):
    segments = parent_row.shape[0]
    seg_index = jnp.arange(segments, dtype=jnp.int32)
    parent_hot = (parent_row[:, None] == seg_index[None, :]).astype(jnp.float32)
    grand_hot = lax.optimization_barrier(jnp.sum(parent_hot[:, :, None] * parent_hot[None, :, :], axis=1))
    identity = (seg_index[:, None] == seg_index[None, :]).astype(jnp.float32)
    ancestry = (identity + parent_hot + grand_hot > 0.5).astype(jnp.float32)
    starts = (jnp.cumsum(length_row) - length_row).astype(jnp.int32)
    before = lax.optimization_barrier(jnp.sum((ancestry - identity) * length_row[None, :].astype(jnp.float32), axis=1))
    places = jnp.arange(tree_len, dtype=jnp.int32)
    segment = lax.optimization_barrier(jnp.sum((places[:, None] >= starts[None, :]).astype(jnp.int32), axis=1)) - 1
    seg_hot = (segment[:, None] == seg_index[None, :]).astype(jnp.float32)
    offset = places.astype(jnp.float32) - lax.optimization_barrier(jnp.sum(seg_hot * starts[None, :].astype(jnp.float32), axis=1))
    position = offset + lax.optimization_barrier(jnp.sum(seg_hot * before[None, :], axis=1))
    return (seg_hot, ancestry, position)

def angles(position):
    half_dim = HEAD_DIM // 2
    exponent = jnp.arange(half_dim, dtype=jnp.float32) * (2.0 / HEAD_DIM)
    inverse = jnp.power(THETA_BASE, -exponent)
    turned = position[:, None] * inverse[None, :]
    turned = jnp.concatenate([turned, turned], axis=1)
    return (jnp.cos(turned), jnp.sin(turned))

def rms_scale(values, gain):
    return values * lax.rsqrt(lax.optimization_barrier(jnp.mean(values * values, axis=-1, keepdims=True)) + EPSILON) * gain

def rotate(values, cosine, sine_table):
    half_dim = values.shape[-1] // 2
    turned = jnp.concatenate([-values[..., half_dim:], values[..., :half_dim]], axis=-1)
    return values * cosine + turned * sine_table

def matmul(left, right):
    return jnp.dot(left, right, precision=lax.Precision.HIGHEST)

def tree_forward(inputs, params, cosine, sine_table, seg_hot, ancestry):
    norm_attn, w_query, w_key, w_value, w_out, norm_ffn, w_gate, w_up, w_down = params
    tree_len = inputs.shape[0]
    group_size = HEADS // KV_HEADS
    normed = low(rms_scale(inputs, low(norm_attn)))
    queries = low_back(matmul(normed, low(w_query)))
    key_rows = low_back(matmul(normed, low(w_key)))
    values = low(low_back(matmul(normed, low(w_value))))
    queries = low(rotate(queries.reshape(tree_len, HEADS, HEAD_DIM), cosine[:, None, :], sine_table[:, None, :]))
    key_rows = low(rotate(key_rows.reshape(tree_len, KV_HEADS, HEAD_DIM), cosine[:, None, :], sine_table[:, None, :]))
    values = values.reshape(tree_len, KV_HEADS, HEAD_DIM)
    queries = queries.reshape(tree_len, KV_HEADS, group_size, HEAD_DIM)
    block_len = min(512, tree_len)
    score_scale = HEAD_DIM ** (-0.5)
    places = jnp.arange(tree_len, dtype=jnp.int32)

    def attend(block_start):
        query_block = lax.dynamic_slice_in_dim(queries, block_start, block_len, 0)
        query_hot = lax.dynamic_slice_in_dim(seg_hot, block_start, block_len, 0)
        allowed = matmul(matmul(query_hot, ancestry), seg_hot.T) > 0.5
        query_place = block_start + jnp.arange(block_len, dtype=jnp.int32)
        allowed = allowed & (places[None, :] <= query_place[:, None])
        scores = low_back(score_scale * jnp.einsum('qgeh,kgh->qgek', query_block, key_rows, precision=lax.Precision.HIGHEST))
        scores = jnp.where(allowed[:, None, None, :], scores, NEGATIVE)
        row_peak = lax.optimization_barrier(jnp.max(scores, axis=-1, keepdims=True))
        log_total = row_peak + jnp.log(lax.optimization_barrier(jnp.sum(jnp.exp(scores - row_peak), axis=-1, keepdims=True)))
        weights = low(jnp.exp(scores - log_total))
        return jnp.einsum('qgek,kgh->qgeh', weights, values, precision=lax.Precision.HIGHEST)
    block_starts = jnp.arange(tree_len // block_len, dtype=jnp.int32) * block_len
    attended = lax.map(jax.checkpoint(attend), block_starts).reshape(tree_len, HEADS * HEAD_DIM)
    attended = low(low_back(attended))
    hidden_state = inputs + low_back(matmul(attended, low(w_out)))
    normed_two = low(rms_scale(hidden_state, low(norm_ffn)))
    gate_value = low_back(matmul(normed_two, low(w_gate)))
    up_value = low_back(matmul(normed_two, low(w_up)))
    activated = low(jax.nn.silu(gate_value) * up_value)
    return hidden_state + low_back(matmul(activated, low(w_down)))

def reference(tokens, parents, lengths, norm_attn, w_query, w_key, w_value, w_out, norm_ffn, w_gate, w_up, w_down, cotangent):
    masters = (norm_attn, w_query, w_key, w_value, w_out, norm_ffn, w_gate, w_up, w_down)

    def per_tree(totals, item):
        tree_tokens, parent_row, length_row, tree_cot = item
        seg_hot, ancestry, position = tree_layout(parent_row, length_row, TREE_LEN)
        cosine, sine_table = angles(position)

        def forward(inputs, params):
            return tree_forward(inputs, params, cosine, sine_table, seg_hot, ancestry)
        result, pull = jax.vjp(forward, tree_tokens.astype(jnp.float32), masters)
        input_grad, param_grads = pull(tree_cot.astype(jnp.float32))
        totals = tuple((running + gradient for running, gradient in zip(totals, param_grads)))
        return (totals, (result.astype(jnp.bfloat16), input_grad))
    zeros = tuple((jnp.zeros(master.shape, jnp.float32) for master in masters))
    totals, stacked = lax.scan(per_tree, zeros, (tokens, parents, lengths, cotangent))
    return (stacked[0], stacked[1], totals[0], totals[1], totals[2], totals[3], totals[4], totals[5], totals[6], totals[7], totals[8])
```

```python
import functools

import jax
import jax.numpy as jnp
from jax import lax
from jax.experimental import pallas as pl
from jax.experimental.pallas import tpu as pltpu
from jax.sharding import PartitionSpec as P

HEADS = 32
KV_HEADS = 4
HEAD_DIM = 64
GROUP = HEADS // KV_HEADS
SCALE = HEAD_DIM ** (-0.5)

EPSILON = 1e-05
NEGATIVE = -1e30
THETA_BASE = 10000.0
BOTH = ("leaf", "seq")
VMEM_LIMIT = 56 * 1024 * 1024

f32 = jnp.float32
bf16 = jnp.bfloat16

NT = (((1,), (1,)), ((), ()))
NN = (((1,), (0,)), ((), ()))
TN = (((0,), (0,)), ((), ()))


def mm(left, right, dims=NN):
    return lax.dot_general(left, right, dims, preferred_element_type=f32)


def after(value, *others):
    return lax.optimization_barrier((value, *others))[0]


def tree_layout(parent_row, length_row, tree_len):
    segments = parent_row.shape[0]
    seg_index = jnp.arange(segments, dtype=jnp.int32)
    parent_hot = (parent_row[:, None] == seg_index[None, :]).astype(f32)
    grand_hot = jnp.sum(parent_hot[:, :, None] * parent_hot[None, :, :], axis=1)
    identity = (seg_index[:, None] == seg_index[None, :]).astype(f32)
    ancestry = (identity + parent_hot + grand_hot > 0.5).astype(f32)
    earlier = seg_index[None, :] < seg_index[:, None]
    starts = jnp.sum(jnp.where(earlier, length_row[None, :], 0), axis=1)
    before = jnp.sum((ancestry - identity) * length_row[None, :].astype(f32), axis=1)
    places = jnp.arange(tree_len, dtype=jnp.int32)
    segment = jnp.sum((places[:, None] >= starts[None, :]).astype(jnp.int32), axis=1) - 1
    seg_hot = (segment[:, None] == seg_index[None, :]).astype(f32)
    offset = places.astype(f32) - jnp.sum(seg_hot * starts[None, :].astype(f32), axis=1)
    position = offset + jnp.sum(seg_hot * before[None, :], axis=1)
    reach = jnp.sum(seg_hot[:, :, None] * ancestry[None, :, :], axis=1)
    return seg_hot, reach, position


def angles(position):
    half_dim = HEAD_DIM // 2
    exponent = jnp.arange(half_dim, dtype=f32) * (2.0 / HEAD_DIM)
    inverse = jnp.power(THETA_BASE, -exponent)
    turned = position[:, None] * inverse[None, :]
    return jnp.cos(turned), jnp.sin(turned)


def turn(values, forward):
    width = values.shape[-1]
    lane = lax.broadcasted_iota(jnp.int32, values.shape, 1)
    low = lane % HEAD_DIM < HEAD_DIM // 2
    ahead = pltpu.roll(values, width - HEAD_DIM // 2, 1)
    behind = pltpu.roll(values, HEAD_DIM // 2, 1)
    if forward:
        return jnp.where(low, -ahead, behind)
    return jnp.where(low, ahead, -behind)


def qkv_kernel(x_ref, gain_ref, w_ref, cos_ref, sin_ref, a_ref, q_ref, kv_ref):
    x = x_ref[...].astype(f32)
    scale = lax.rsqrt(jnp.mean(x * x, axis=-1, keepdims=True) + EPSILON)
    a = (x * scale * gain_ref[...]).astype(bf16)
    a_ref[...] = a
    rows = mm(a, w_ref[...])
    cos, sin = cos_ref[...], sin_ref[...]
    q_width = q_ref.shape[1]
    for j in range(q_width // 128):
        u = rows[:, j * 128 : (j + 1) * 128]
        q_ref[:, j * 128 : (j + 1) * 128] = (
            (u * cos + turn(u, True) * sin).astype(bf16) * jnp.array(SCALE, bf16)
        )
    u = rows[:, q_width:]
    lane = lax.broadcasted_iota(jnp.int32, u.shape, 1)
    kv_ref[...] = jnp.where(lane < HEAD_DIM, u * cos + turn(u, True) * sin, u).astype(bf16)


def project(x, gain, weight, cos, sin):
    tokens, width = x.shape
    q_width = weight.shape[1] - 2 * HEAD_DIM
    block = min(256, tokens)
    row = lambda i: (i, 0)
    whole = lambda i: (0, 0)
    return pl.pallas_call(
        qkv_kernel,
        grid=(tokens // block,),
        in_specs=[
            pl.BlockSpec((block, width), row),
            pl.BlockSpec((1, width), whole),
            pl.BlockSpec(weight.shape, whole),
            pl.BlockSpec((block, 128), row),
            pl.BlockSpec((block, 128), row),
        ],
        out_specs=[
            pl.BlockSpec((block, width), row),
            pl.BlockSpec((block, q_width), row),
            pl.BlockSpec((block, 128), row),
        ],
        out_shape=[
            jax.ShapeDtypeStruct((tokens, width), bf16),
            jax.ShapeDtypeStruct((tokens, q_width), bf16),
            jax.ShapeDtypeStruct((tokens, 128), bf16),
        ],
        compiler_params=pltpu.CompilerParams(vmem_limit_bytes=VMEM_LIMIT),
        cost_estimate=pl.CostEstimate(
            flops=2 * tokens * width * weight.shape[1],
            bytes_accessed=4 * tokens * width + 2 * weight.size,
            transcendentals=0,
        ),
    )(x, gain, weight, cos, sin)


def half_masks():
    lane = lax.broadcasted_iota(jnp.int32, (1, 128), 1)
    low = jnp.where(lane < HEAD_DIM, 1.0, 0.0).astype(bf16)
    high = jnp.where(lane < HEAD_DIM, 0.0, 1.0).astype(bf16)
    return low, high


def fill_bias(bias_ref, hot_ref, reach_ref, place_ref, first, block, keys):
    seen = mm(hot_ref[:keys, :], reach_ref[first : first + block, :], NT)
    key_place = lax.broadcasted_iota(jnp.int32, (keys, block), 0)
    allowed = (seen > 0.5) & (key_place <= place_ref[:, first : first + block])
    bias_ref[:keys, :] = jnp.where(allowed, 0.0, NEGATIVE)


def attend_kernel(
    block, q_ref, kv_ref, vk_ref, vt_ref, hot_ref, reach_ref, place_ref, o_ref, lse_ref, bias_ref
):
    tokens, q_width = q_ref.shape
    masks = half_masks()
    for t in range(tokens // block):
        first, keys = t * block, (t + 1) * 2 * block
        fill_bias(bias_ref, hot_ref, reach_ref, place_ref, first, block, keys)

        def pair(j, carry, first=first, keys=keys):
            columns = pl.ds(pl.multiple_of(j * 128, 128), 128)
            both = q_ref[first : first + block, columns]
            outs = []
            for a in range(2):
                k_ref = (kv_ref, vk_ref)[a]
                s = mm(k_ref[:keys, :], both * masks[a], NT) + bias_ref[:keys, :]
                peak = jnp.max(s, axis=0, keepdims=True)
                e = jnp.exp(s - peak)
                total = jnp.sum(e, axis=0, keepdims=True)
                outs.append(mm(vt_ref[:, :keys], e.astype(bf16)) * (1.0 / total))
                lse_ref[j, a : a + 1, first : first + block] = peak + jnp.log(total)
            o_ref[first : first + block, columns] = jnp.concatenate(outs, axis=0).T.astype(bf16)
            return carry

        lax.fori_loop(0, q_width // 128, pair, 0)


def attend(q, kv, vk, vt, hot, reach, place, block):
    tokens, q_width = q.shape
    keys = kv.shape[0]
    pairs = q_width // 128
    return pl.pallas_call(
        functools.partial(attend_kernel, block),
        out_shape=[
            jax.ShapeDtypeStruct((tokens, q_width), bf16),
            jax.ShapeDtypeStruct((pairs, 2, tokens), f32),
        ],
        scratch_shapes=[pltpu.VMEM((keys, block), f32)],
        compiler_params=pltpu.CompilerParams(vmem_limit_bytes=VMEM_LIMIT),
        cost_estimate=pl.CostEstimate(
            flops=10 * tokens * keys * q_width, bytes_accessed=4 * tokens * q_width, transcendentals=0
        ),
    )(q, kv, vk, vt, hot, reach, place)


def pull_kernel(
    block,
    q_ref,
    g_ref,
    lse_ref,
    kv_ref,
    vk_ref,
    kt_ref,
    hot_ref,
    reach_ref,
    place_ref,
    cos_ref,
    sin_ref,
    dq_ref,
    one_ref,
    two_ref,
    bias_ref,
):
    tokens, q_width = q_ref.shape
    masks = half_masks()
    one_ref[...] = jnp.zeros_like(one_ref)
    two_ref[...] = jnp.zeros_like(two_ref)
    for t in range(tokens // block):
        first, keys = t * block, (t + 1) * 2 * block
        fill_bias(bias_ref, hot_ref, reach_ref, place_ref, first, block, keys)
        cos, sin = cos_ref[first : first + block, :], sin_ref[first : first + block, :]

        def pair(j, carry, first=first, keys=keys, cos=cos, sin=sin):
            columns = pl.ds(pl.multiple_of(j * 128, 128), 128)
            q_both = q_ref[first : first + block, columns]
            g_both = g_ref[first : first + block, columns]
            outs = []
            for a in range(2):
                k_ref = (kv_ref, vk_ref)[a]
                v_ref = (vk_ref, kv_ref)[a]
                q, g = q_both * masks[a], g_both * masks[a]
                s = mm(k_ref[:keys, :], q, NT) + bias_ref[:keys, :]
                p = jnp.exp(s - lse_ref[j, a : a + 1, first : first + block])
                dp = mm(v_ref[:keys, :], g, NT)
                delta = jnp.sum(p * dp, axis=0, keepdims=True)
                ds = (p * (dp - delta)).astype(bf16)
                outs.append(mm(kt_ref[:, :keys], ds))
                k_sum, v_sum = ((one_ref, two_ref), (two_ref, one_ref))[a]
                k_sum[:keys, :] += mm(ds, q)
                v_sum[:keys, :] += mm(p.astype(bf16), g)
            dq = jnp.concatenate(outs, axis=0).T * SCALE
            dq_ref[first : first + block, columns] = (
                dq * cos + turn(dq * sin, False)
            ).astype(bf16)
            return carry

        lax.fori_loop(0, q_width // 128, pair, 0)


def pull(q, g, lse, kv, vk, kt, hot, reach, place, cos, sin, block):
    tokens, q_width = q.shape
    keys = kv.shape[0]
    return pl.pallas_call(
        functools.partial(pull_kernel, block),
        out_shape=[
            jax.ShapeDtypeStruct((tokens, q_width), bf16),
            jax.ShapeDtypeStruct((keys, 128), f32),
            jax.ShapeDtypeStruct((keys, 128), f32),
        ],
        scratch_shapes=[pltpu.VMEM((keys, block), f32)],
        compiler_params=pltpu.CompilerParams(vmem_limit_bytes=VMEM_LIMIT),
        cost_estimate=pl.CostEstimate(
            flops=24 * tokens * keys * q_width, bytes_accessed=8 * tokens * q_width, transcendentals=0
        ),
    )(q, g, lse, kv, vk, kt, hot, reach, place, cos, sin)


class Place:
    def __init__(self):
        self.leaves, self.seqs = lax.axis_size("leaf"), lax.axis_size("seq")
        self.lines = self.seqs // 2
        leaf, seq = lax.axis_index("leaf"), lax.axis_index("seq")
        self.leaf = leaf
        self.far, self.core, self.line, self.near = leaf // 2, leaf % 2, seq // 2, seq % 2
        self.core_pairs = [(i, i ^ 1) for i in range(self.leaves)]
        self.far_pairs = [(i, i ^ 2) for i in range(self.leaves)]
        self.near_pairs = [(i, i ^ 1) for i in range(self.seqs)]
        self.square = [[], []]
        for i in range(self.leaves):
            for j in range(self.seqs):
                here = i * self.seqs + j
                far, near = (i ^ 2) * self.seqs + j, i * self.seqs + (j ^ 1)
                self.square[0].append((here, near if i % 2 else far))
                self.square[1].append((here, far if i % 2 else near))

    def shift(self, value, step, only=None):
        pairs = [
            ((a * 2 + b), (a + step) * 2 + b)
            for a in range(self.lines)
            for b in range(2)
            if 0 <= a + step < self.lines and (only is None or only(a))
        ]
        return lax.ppermute(value, "seq", pairs)

    def pick(self, stack, index, axis=0):
        return lax.dynamic_index_in_dim(stack, index, axis, keepdims=False)

    def in_order(self, ups, own, downs):
        stack = jnp.stack([*ups[::-1], own, *downs])
        return lax.dynamic_slice_in_dim(stack, self.lines - 1 - self.line, self.lines, 0)

    def line_gather(self, value):
        ups, downs = [value], [value]
        for _ in range(self.lines - 1):
            ups.append(self.shift(ups[-1], 1))
            downs.append(self.shift(downs[-1], -1))
        return self.in_order(ups[1:], value, downs[1:])

    def line_sum(self, parts):
        last = self.lines - 1
        up = down = None
        for j in range(last):
            mine_up = self.pick(parts, jnp.minimum(self.line + last - j, last))
            mine_down = self.pick(parts, jnp.maximum(self.line - last + j, 0))
            if up is not None:
                mine_up = (mine_up.astype(f32) + up.astype(f32)).astype(bf16)
                mine_down = (mine_down.astype(f32) + down.astype(f32)).astype(bf16)
            up = self.shift(mine_up, 1, lambda a, j=j: a <= j)
            down = self.shift(mine_down, -1, lambda a, j=j: a >= last - j)
        own = self.pick(parts, self.line).astype(f32)
        return own + up.astype(f32) + down.astype(f32)

    def line_swap(self, parts):
        ups, downs = [], []
        last = self.lines - 1
        for d in range(1, self.lines):
            ups.append(self.shift(self.pick(parts, jnp.minimum(self.line + d, last)), d))
            downs.append(self.shift(self.pick(parts, jnp.maximum(self.line - d, 0)), -d))
        return self.in_order(ups, self.pick(parts, self.line), downs)

    def square_gather(self, piece, axis):
        first = lax.ppermute(piece, BOTH, self.square[0])
        two = jnp.stack([piece, first])
        second = lax.ppermute(two, BOTH, self.square[1])
        four = jnp.concatenate([two, second])
        other = lax.ppermute(four, "leaf", self.core_pairs)
        pieces = []
        for near in range(2):
            for far in range(2):
                to_near, to_far = near ^ self.near, far ^ self.far
                for core in range(2):
                    index = (to_near * 2 + to_far) if core == 0 else (to_far * 2 + to_near)
                    pieces.append(
                        jnp.where(
                            self.core == core, self.pick(four, index), self.pick(other, index)
                        )
                    )
        return jnp.stack(pieces, axis)

    def square_sum(self, parts, axis):
        shape = parts.shape
        split = parts.reshape(shape[:axis] + (4, 2) + shape[axis + 1 :])
        give = self.pick(split, 1 - self.core, axis + 1)
        keep = self.pick(split, self.core, axis + 1)
        got = lax.ppermute(give, "leaf", self.core_pairs)
        four = (keep.astype(f32) + got.astype(f32)).astype(bf16)
        four = four.reshape(shape[:axis] + (2, 2) + shape[axis + 1 :])

        def side(near, far):
            return jnp.where(
                self.core == 0, self.pick(four, near, axis), self.pick(four, far, axis + 1)
            )

        got = lax.ppermute(side(1 - self.near, 1 - self.far), BOTH, self.square[1])
        two = (side(self.near, self.far).astype(f32) + got.astype(f32)).astype(bf16)
        rest = jnp.where(self.core == 0, self.far, self.near)
        got = lax.ppermute(self.pick(two, 1 - rest, axis), BOTH, self.square[0])
        return (self.pick(two, rest, axis).astype(f32) + got.astype(f32)).astype(bf16)

    def leaf_gather(self, value):
        far = lax.ppermute(value, "leaf", self.far_pairs)
        two = jnp.where(
            self.far == 0, jnp.stack([value, far]), jnp.stack([far, value])
        )
        other = lax.ppermute(two, "leaf", self.core_pairs)
        pair = jnp.where(
            self.core == 0, jnp.stack([two, other], 1), jnp.stack([other, two], 1)
        )
        return pair.reshape((4,) + value.shape)

    def sum_all(self, value):
        for axis, pairs in (
            ("leaf", self.core_pairs),
            ("leaf", self.far_pairs),
            ("seq", self.near_pairs),
        ):
            value = value + lax.ppermute(value, axis, pairs)
        return jnp.sum(self.line_gather(value), axis=0)


def rms_back(values, gain, grad):
    scale = lax.rsqrt(jnp.mean(values * values, axis=-1, keepdims=True) + EPSILON)
    inner = grad * gain
    mean = jnp.mean(inner * values, axis=-1, keepdims=True)
    return scale * inner - values * (scale * scale * scale * mean)


def on_device(
    tokens,
    parents,
    lengths,
    norm_attn,
    w_query,
    w_key,
    w_value,
    w_out,
    norm_ffn,
    w_gate,
    w_up,
    w_down,
    cotangent,
):
    at = Place()
    lines = at.lines
    _, block, width = tokens.shape
    tree_len = block * at.seqs
    rows = w_query.shape[0]
    quarter = rows // 4
    hidden = w_gate.shape[1] // lines
    heads = HEADS // lines
    q_width = heads * HEAD_DIM
    own_tokens = lines * block
    kv_of = [(i * heads) // GROUP for i in range(lines)]

    x_home = tokens[0]
    dy_home = cotangent[0]

    def quarter_of(weight):
        return lax.dynamic_slice_in_dim(weight, at.leaf * (weight.shape[0] // 4), weight.shape[0] // 4, 0)

    def columns(weight, size):
        return quarter_of(weight).astype(bf16).reshape(-1, lines, size).transpose(1, 0, 2)

    def kv_columns(weight):
        low = quarter_of(weight).astype(bf16)
        return jnp.stack([low[:, i * HEAD_DIM : (i + 1) * HEAD_DIM] for i in kv_of])

    x_all = at.line_gather(x_home)
    gains_low = jnp.stack([norm_attn.astype(bf16), norm_ffn.astype(bf16)])
    gains_near = lax.ppermute(gains_low, "seq", at.near_pairs)
    gains_two = jnp.where(
        at.near == 0, jnp.stack([gains_low, gains_near], 1), jnp.stack([gains_near, gains_low], 1)
    )
    gains = at.line_gather(gains_two).transpose(1, 0, 2, 3).reshape(2, width).astype(f32)
    gain_one, gain_two = gains[0:1], gains[1:2]

    qkv_parts = jnp.concatenate(
        [columns(w_query, q_width), kv_columns(w_key), kv_columns(w_value)], axis=2
    )
    qkv_weight = at.square_gather(at.line_swap(qkv_parts), 1).reshape(width, -1)

    seg_hot, reach, position = tree_layout(parents[0], lengths[0], tree_len)
    pad = 128 - seg_hot.shape[1]
    hot_low = jnp.pad(seg_hot, ((0, 0), (0, pad))).astype(bf16)
    spread = lambda a: at.pick(a.reshape((lines, 2, block) + a.shape[1:]), at.near, 1).reshape(
        (own_tokens,) + a.shape[1:]
    )
    reach_own = spread(jnp.pad(reach, ((0, 0), (0, pad))).astype(bf16))
    place_own = spread(jnp.arange(tree_len, dtype=jnp.int32))[None, :]
    cos, sin = angles(spread(position))
    cos, sin = jnp.tile(cos, (1, 4)), jnp.tile(sin, (1, 4))

    x_rows = x_all.reshape(own_tokens, width)
    a_one, q, kv_own = project(x_rows, gain_one, qkv_weight, cos, sin)
    kv_near = lax.ppermute(kv_own, "seq", at.near_pairs)
    own_kv, near_kv = kv_own.reshape(lines, block, 128), kv_near.reshape(lines, block, 128)
    kv = jnp.where(
        at.near == 0, jnp.stack([own_kv, near_kv], 1), jnp.stack([near_kv, own_kv], 1)
    ).reshape(tree_len, 128)
    vk = jnp.concatenate([kv[:, HEAD_DIM:], kv[:, :HEAD_DIM]], axis=1)
    kv_t = kv.T
    attended, lse = attend(q, kv, vk, kv_t[HEAD_DIM:], hot_low, reach_own, place_own, block)

    out_weight = at.square_gather(quarter_of(w_out).astype(bf16), 0).reshape(q_width, width)
    gate_up_parts = jnp.concatenate([columns(w_gate, hidden), columns(w_up, hidden)], axis=2)
    gate_up_parts = after(gate_up_parts, x_all)
    gate_up_weight = at.square_gather(at.line_swap(gate_up_parts), 1).reshape(width, 2 * hidden)
    down_weight = at.square_gather(quarter_of(w_down).astype(bf16), 0).reshape(hidden, width)

    out_parts = mm(attended, out_weight).astype(bf16).reshape(lines, block, width)
    state = x_home.astype(f32) + at.line_sum(out_parts)
    state_scale = lax.rsqrt(jnp.mean(state * state, axis=-1, keepdims=True) + EPSILON)
    second_home = (state * state_scale * gain_two).astype(bf16)
    second = at.line_gather(second_home).reshape(own_tokens, width)
    dy_home = after(dy_home, second_home)
    dy = at.line_gather(dy_home).reshape(own_tokens, width)

    gate_up = mm(second, gate_up_weight)
    gate, up = gate_up[:, :hidden], gate_up[:, hidden:]
    sigmoid = jax.nn.sigmoid(gate)
    silu = gate * sigmoid
    activated = (silu * up).astype(bf16)
    down_parts = mm(activated, down_weight).astype(bf16).reshape(lines, block, width)
    d_act = mm(dy, down_weight, NT)
    d_gate = (d_act * up * (sigmoid * (1.0 + gate * (1.0 - sigmoid)))).astype(bf16)
    d_up = (d_act * silu).astype(bf16)
    d_gate_up = jnp.concatenate([d_gate, d_up], axis=1)
    second_parts = mm(d_gate_up, gate_up_weight, NT).astype(bf16).reshape(lines, block, width)
    d_second = at.line_sum(second_parts)
    state_grad = dy_home.astype(f32) + rms_back(state, gain_two, d_second)
    gain_two_terms = jnp.sum(d_second * state * state_scale, axis=0)
    state_low = state_grad.astype(bf16)
    state_all = at.line_gather(state_low).reshape(own_tokens, width)

    down_parts = after(down_parts, state_all)
    output = (state + at.line_sum(down_parts)).astype(bf16)

    gate_up_grad = mm(second, d_gate_up, TN).astype(bf16)
    down_grad = mm(activated, dy, TN).astype(bf16)

    d_att = mm(state_all, out_weight, NT).astype(bf16)
    out_grad = mm(attended, state_all, TN).astype(bf16)
    dq, one, two = pull(
        q, d_att, lse, kv, vk, kv_t[:HEAD_DIM], hot_low, reach_own, place_own, cos, sin, block
    )
    d_kv = jnp.concatenate(
        [one[:, :HEAD_DIM] + two[:, HEAD_DIM:], one[:, HEAD_DIM:] + two[:, :HEAD_DIM]], axis=1
    ).reshape(lines, 2, block, 128)
    kv_got = lax.ppermute(at.pick(d_kv, 1 - at.near, 1).astype(bf16), "seq", at.near_pairs)
    d_kv = (at.pick(d_kv, at.near, 1) + kv_got.astype(f32)).reshape(own_tokens, 128)
    d_k, d_v = d_kv[:, :HEAD_DIM], d_kv[:, HEAD_DIM:]
    half = HEAD_DIM // 2
    turned = d_k * sin[:, :HEAD_DIM]
    d_k = d_k * cos[:, :HEAD_DIM] + jnp.concatenate([turned[:, half:], -turned[:, :half]], axis=1)
    d_qkv = jnp.concatenate([dq, d_k.astype(bf16), d_v.astype(bf16)], axis=1)
    first_wide = mm(d_qkv, qkv_weight, NT)
    x_wide = x_rows.astype(f32)
    x_scale = lax.rsqrt(jnp.mean(x_wide * x_wide, axis=-1, keepdims=True) + EPSILON)
    gain_one_terms = jnp.sum(first_wide * x_wide * x_scale, axis=0)
    d_first = at.line_sum(first_wide.astype(bf16).reshape(lines, block, width))
    input_grad = state_grad + rms_back(x_home.astype(f32), gain_one, d_first)
    qkv_grad = mm(a_one, d_qkv, TN).astype(bf16)

    def rows_home(grad):
        mine = at.square_sum(grad.reshape(8, -1, grad.shape[1]), 0)
        return at.leaf_gather(mine).reshape(-1, grad.shape[1])

    def columns_home(grad):
        mine = at.square_sum(grad.reshape(lines, 8, quarter, grad.shape[1]), 1)
        mine = at.line_swap(mine)
        return at.leaf_gather(mine.transpose(1, 0, 2)).reshape(rows, lines, grad.shape[1])

    grad_down = rows_home(down_grad).astype(f32)
    gate_up_home = columns_home(gate_up_grad)
    grad_gate = gate_up_home[:, :, :hidden].reshape(rows, -1).astype(f32)
    grad_up = gate_up_home[:, :, hidden:].reshape(rows, -1).astype(f32)
    grad_out = rows_home(out_grad).astype(f32)
    qkv_home = columns_home(qkv_grad)
    grad_query = qkv_home[:, :, :q_width].reshape(rows, -1).astype(f32)

    def kv_home(part):
        terms = [[] for _ in range(KV_HEADS)]
        for i in range(lines):
            terms[kv_of[i]].append(part[:, i, :].astype(f32))
        return jnp.concatenate([functools.reduce(jnp.add, t) for t in terms], axis=1)

    grad_key = kv_home(qkv_home[:, :, q_width : q_width + HEAD_DIM])
    grad_value = kv_home(qkv_home[:, :, q_width + HEAD_DIM :])
    gain_sums = at.sum_all(jnp.stack([gain_one_terms, gain_two_terms]))
    gain_grads = lax.dynamic_slice_in_dim(
        gain_sums, lax.axis_index("seq") * rows, rows, 1
    )
    return (
        output[None],
        input_grad[None],
        gain_grads[0],
        grad_query,
        grad_key,
        grad_value,
        grad_out,
        gain_grads[1],
        grad_gate,
        grad_up,
        grad_down,
    )


def solution(mesh):
    return jax.shard_map(
        on_device,
        mesh=mesh,
        in_specs=(
            P("leaf", "seq", None),
            P("leaf", None),
            P("leaf", None),
            P("seq"),
            P("seq", None),
            P("seq", None),
            P("seq", None),
            P("seq", None),
            P("seq"),
            P("seq", None),
            P("seq", None),
            P("seq", None),
            P("leaf", "seq", None),
        ),
        out_specs=(
            P("leaf", "seq", None),
            P("leaf", "seq", None),
            P("seq"),
            P("seq", None),
            P("seq", None),
            P("seq", None),
            P("seq", None),
            P("seq"),
            P("seq", None),
            P("seq", None),
            P("seq", None),
        ),
        check_vma=False,
    )
```
